32 devices in a mesh: rows: 8 (over z, x), chan: 4 (over y, core).
Axes of the slice: x: 2, y: 2, z: 4, core: 2. Of those that a mesh axis runs over, the one named last changes fastest.
Arguments:
- inputs: bfloat16 [256, 16, 1024], P('chan', 'rows'), may hold values from -6 to 6
- kernel: bfloat16 [256, 2304], replicated, may hold values from -0.125 to 0.125
- out_grad: bfloat16 [256, 16, 1024], P('chan', 'rows'), may hold values from -6 to 6
Outputs:
- outputs: bfloat16 [256, 16, 1024], P('chan', 'rows')
- in_grad: bfloat16 [256, 16, 1024], P('chan', 'rows')
- kernel_grad: float32 [256, 2304], P('chan', 'rows')
The draws below stay inside these ranges and needn't reach their ends.
All inputs are finite; a program needn't handle non-finite values.
Results may differ from the reference program's by a relative error of at most 0.00105.
Values may be sent and summed in bfloat16 or wider, within the bound.
A program may use at most 64 MiB of HBM per device.

```python
import math
import jax
import jax.numpy as jnp
from jax import lax

C = 256
WID = 1024
NH = 16


def block_levels(own_key, extent, cuts, least, high):
    gain, own = 1.0, jax.random.fold_in(own_key, 6)
    for axis_at, shards_of in cuts:
        steps = jnp.exp(jax.random.uniform(jax.random.fold_in(own, axis_at), (shards_of,), jnp.float32, least / len(cuts), high / len(cuts)))
        gain = gain * jnp.repeat(steps, extent[axis_at] // shards_of).reshape([-1 if axis == axis_at else 1 for axis in range(len(extent))])
    return gain


def normal_values(stream_key, dims, width, reach, split=(), kind=jnp.bfloat16):
    entries = jax.random.normal(stream_key, dims, jnp.float32) * width
    if len(split) > 0:
        entries = block_levels(stream_key, dims, split, -0.22, 0.18) * entries
    return jnp.clip(entries, min=-reach, max=reach).astype(kind)


def setup_inputs(seed: int = 0) -> dict:
    key_of = jax.random.split(jax.random.key(seed), 4)
    inputs = normal_values(key_of[0], (C, NH, WID), 1.0, 6.0, ((0, 4), (1, 8)))
    kernel = normal_values(key_of[1], (C, 9 * C), (9 * C) ** -0.5, 0.125)
    out_grad = normal_values(key_of[2], (C, NH, WID), 1.0, 6.0, ((0, 4), (1, 8)))
    return {"inputs": inputs, "kernel": kernel, "out_grad": out_grad}


def convolve(source, filters, specs, padding):
    return lax.conv_general_dilated(source, filters, (1, 1), padding, dimension_numbers=specs, precision=lax.Precision.HIGHEST, preferred_element_type=jnp.float32)

def reference(inputs, kernel, out_grad):
    channels = inputs.shape[0]
    fields = inputs.astype(jnp.float32)[None]
    grads = out_grad.astype(jnp.float32)[None]
    taps = kernel.astype(jnp.float32).reshape(channels, 3, 3, channels)
    forward = convolve(fields, taps, ('NCHW', 'OHWI', 'NCHW'), ((1, 1), (1, 1)))[0]
    flipped = taps[:, ::-1, ::-1, :]
    backward = convolve(grads, flipped, ('NCHW', 'IHWO', 'NCHW'), ((1, 1), (1, 1)))[0]
    kernel_terms = convolve(fields, grads, ('CNHW', 'IOHW', 'CNHW'), ((1, 1), (1, 1)))
    scale = 1.0 / math.sqrt(NH * WID)
    kernel_grad = jnp.transpose(kernel_terms, (0, 2, 3, 1)).reshape(channels, 9 * channels) * scale
    return (forward.astype(jnp.bfloat16), backward.astype(jnp.bfloat16), kernel_grad)
```

```python
import functools
import math

import jax
import jax.numpy as jnp
from jax import lax
from jax.experimental import pallas as pl
from jax.experimental.pallas import tpu as pltpu
from jax.sharding import PartitionSpec as P

MESH = pl.DeviceIdType.MESH

OWN, UP, DOWN = 0, 1, 2


def shifted(x, by):
    width = x.shape[1]
    at = lax.broadcasted_iota(jnp.int32, x.shape, 1)
    edge = 0 if by > 0 else width - 1
    return jnp.where(at == edge, 0.0, pltpu.roll(x, by % width, 1))


def kernel(
    strips, scale, x_ref, g_ref, wf_ref, wb_ref, out_ref, ing_ref, kg_ref,
    x_buf, g_buf, taps_g, whole, pieces, landed, send_sem, recv_sem, kg_send, kg_recv, local_sem,
):
    own, height = x_ref.shape[1], x_ref.shape[0]
    channels = x_buf.shape[1]
    width = x_ref.shape[2]
    piece = kg_ref.shape[1]
    row = lax.axis_index("rows")
    chan = lax.axis_index("chan")
    sibling = chan + 1 - 2 * lax.rem(chan, 2)
    across = lax.rem(chan + 2, 4)
    diagonal = lax.rem(sibling + 2, 4)
    of = (chan, sibling, across, diagonal)
    bufs = (x_buf, g_buf)
    last = strips - 1
    span = {OWN: (1, height), UP: (0, 1), DOWN: (height + 1, 1)}

    def region(t, kind, channel):
        start, count = span[kind]
        return bufs[t].at[pl.ds(start, count), pl.ds(pl.multiple_of(channel * own, own), own), :]

    def relay(t, kind, held, to):
        where = region(t, kind, of[held])
        return pltpu.make_async_remote_copy(
            src_ref=where, dst_ref=where,
            send_sem=send_sem.at[t, kind, held ^ to], recv_sem=recv_sem.at[t, kind, held ^ to],
            device_id=(row, of[to]), device_id_type=MESH,
        )

    def edge(t, kind):
        at, to = (height, row + 1) if kind == UP else (1, row - 1)
        return pltpu.make_async_remote_copy(
            src_ref=bufs[t].at[pl.ds(at, 1), pl.ds(pl.multiple_of(chan * own, own), own), :],
            dst_ref=region(t, kind, chan),
            send_sem=send_sem.at[t, kind, 0], recv_sem=recv_sem.at[t, kind, 0],
            device_id=(to, chan), device_id_type=MESH,
        )

    def arrived(t, kind, held):
        where = region(t, kind, of[held])
        pltpu.make_async_remote_copy(
            src_ref=where, dst_ref=where,
            send_sem=send_sem.at[t, kind, held], recv_sem=recv_sem.at[t, kind, held],
            device_id=(row, sibling), device_id_type=MESH,
        ).wait_recv()

    has = {UP: row > 0, DOWN: row < last}
    feeds = {UP: row < last, DOWN: row > 0}

    mine = [
        pltpu.make_async_copy((x_ref, g_ref)[t], region(t, OWN, chan), local_sem.at[t])
        for t in range(2)
    ]
    for copy in mine:
        copy.start()

    barrier = pltpu.get_barrier_semaphore()
    for peer in (sibling, across):
        pl.semaphore_signal(barrier, inc=1, device_id=(row, peer), device_id_type=MESH)

    @pl.loop(1, strips)
    def _(d):
        pl.semaphore_signal(
            barrier, inc=1, device_id=(lax.rem(row + d, strips), chan), device_id_type=MESH
        )

    for kind, at in ((UP, 0), (DOWN, height + 1)):

        @pl.when(jnp.logical_not(has[kind]))
        def _():
            for t in range(2):
                bufs[t][at] = jnp.zeros((channels, width), jnp.bfloat16)

    for copy in mine:
        copy.wait()
    pl.semaphore_wait(barrier, strips + 1)

    for t in range(2):
        for kind in (UP, DOWN):

            @pl.when(feeds[kind])
            def _():
                edge(t, kind).start()

        relay(t, OWN, 0, 2).start()
        relay(t, OWN, 0, 1).start()

    for h in range(height):
        rows = g_ref[h].astype(jnp.float32)
        taps_g[h, 0:own] = shifted(rows, -1).astype(jnp.bfloat16)
        taps_g[h, own : 2 * own] = g_ref[h]
        taps_g[h, 2 * own : 3 * own] = shifted(rows, 1).astype(jnp.bfloat16)

    for t in range(2):
        for kind in (UP, DOWN):

            @pl.when(has[kind])
            def _():
                arrived(t, kind, 0)
                relay(t, kind, 0, 2).start()
                relay(t, kind, 0, 1).start()

        arrived(t, OWN, 2)
        relay(t, OWN, 2, 1).start()

    def pass_on(t):
        for kind in (UP, DOWN):

            @pl.when(has[kind])
            def _():
                arrived(t, kind, 2)
                relay(t, kind, 2, 1).start()

    def complete(t):
        arrived(t, OWN, 1)
        arrived(t, OWN, 3)
        for kind in (UP, DOWN):

            @pl.when(has[kind])
            def _():
                arrived(t, kind, 1)
                arrived(t, kind, 3)

    def stack(t, h):
        return bufs[t][h : h + 3].reshape(3 * channels, width)

    def convolve(t, w_ref, to_ref):
        for h in range(height):
            terms = jnp.dot(w_ref[...], stack(t, h), preferred_element_type=jnp.float32)
            total = (
                shifted(terms[0:own], 1) + terms[own : 2 * own] + shifted(terms[2 * own : 3 * own], -1)
            )
            to_ref[h] = total.astype(to_ref.dtype)

    pass_on(0)
    complete(0)
    terms = None
    for h in range(height):
        term = lax.dot_general(
            taps_g[h], stack(0, h), (((1,), (1,)), ((), ())), preferred_element_type=jnp.float32
        )
        terms = term if terms is None else terms + term
    for a in range(3):
        for b in range(3):
            whole[:, (3 * a + b) * channels : (3 * a + b + 1) * channels] = (
                terms[b * own : (b + 1) * own, a * channels : (a + 1) * channels] * scale
            )
    for s in range(strips):
        pieces[s] = whole[:, s * piece : (s + 1) * piece]

    def share(d):
        to = lax.rem(row + d, strips)
        return pltpu.make_async_remote_copy(
            src_ref=pieces.at[to], dst_ref=landed.at[d],
            send_sem=kg_send.at[d], recv_sem=kg_recv.at[d],
            device_id=(to, chan), device_id_type=MESH,
        )

    @pl.loop(1, strips)
    def _(d):
        share(d).start()

    pass_on(1)
    convolve(0, wf_ref, out_ref)
    complete(1)
    convolve(1, wb_ref, ing_ref)

    kg_ref[...] = pieces[row]

    @pl.loop(1, strips)
    def _(d):
        share(d).wait_recv()
        kg_ref[...] += landed[d]

    @pl.loop(1, strips)
    def _(d):
        share(d).wait_send()

    for t in range(2):
        relay(t, OWN, 0, 2).wait_send()
        relay(t, OWN, 0, 1).wait_send()
        relay(t, OWN, 2, 1).wait_send()
        for kind in (UP, DOWN):

            @pl.when(feeds[kind])
            def _():
                edge(t, kind).wait_send()

            @pl.when(has[kind])
            def _():
                relay(t, kind, 0, 2).wait_send()
                relay(t, kind, 0, 1).wait_send()
                relay(t, kind, 2, 1).wait_send()


def body(inputs, kernel_taps, out_grad):
    channels = kernel_taps.shape[0]
    own, height, width = inputs.shape
    strips = lax.axis_size("rows")
    piece = 9 * channels // strips
    first = lax.axis_index("chan") * own
    taps = kernel_taps.reshape(channels, 3, 3, channels)
    forward = lax.dynamic_slice_in_dim(taps, first, own, 0)
    forward = jnp.transpose(forward, (2, 0, 1, 3)).reshape(3 * own, 3 * channels)
    backward = lax.dynamic_slice_in_dim(taps, first, own, 3)[:, ::-1, ::-1, :]
    backward = jnp.transpose(backward, (2, 3, 1, 0)).reshape(3 * own, 3 * channels)
    scale = 1.0 / math.sqrt(height * strips * width)
    block = jax.ShapeDtypeStruct((height, own, width), jnp.bfloat16)
    vmem = pl.BlockSpec(memory_space=pltpu.VMEM)
    outputs, in_grad, kernel_grad = pl.pallas_call(
        functools.partial(kernel, strips, scale),
        out_shape=(block, block, jax.ShapeDtypeStruct((own, piece), jnp.float32)),
        in_specs=[vmem] * 4,
        out_specs=(vmem,) * 3,
        scratch_shapes=[
            pltpu.VMEM((height + 2, channels, width), jnp.bfloat16),
            pltpu.VMEM((height + 2, channels, width), jnp.bfloat16),
            pltpu.VMEM((height, 3 * own, width), jnp.bfloat16),
            pltpu.VMEM((own, 9 * channels), jnp.float32),
            pltpu.VMEM((strips, own, piece), jnp.float32),
            pltpu.VMEM((strips, own, piece), jnp.float32),
            pltpu.SemaphoreType.DMA((2, 3, 4)),
            pltpu.SemaphoreType.DMA((2, 3, 4)),
            pltpu.SemaphoreType.DMA((strips,)),
            pltpu.SemaphoreType.DMA((strips,)),
            pltpu.SemaphoreType.DMA((2,)),
        ],
        compiler_params=pltpu.CompilerParams(
            collective_id=0, has_side_effects=True, vmem_limit_bytes=40 * 1024 * 1024
        ),
    )(jnp.transpose(inputs, (1, 0, 2)), jnp.transpose(out_grad, (1, 0, 2)), forward, backward)
    return (jnp.transpose(outputs, (1, 0, 2)), jnp.transpose(in_grad, (1, 0, 2)), kernel_grad)


def solution(mesh):
    placed = (P("chan", "rows", None), P(), P("chan", "rows", None))
    return jax.shard_map(
        body,
        mesh=mesh,
        in_specs=placed,
        out_specs=(P("chan", "rows", None), P("chan", "rows", None), P("chan", "rows")),
        check_vma=False,
    )
```

```python
import functools
import math

import jax
import jax.numpy as jnp
from jax import lax
from jax.experimental import pallas as pl
from jax.experimental.pallas import tpu as pltpu
from jax.sharding import PartitionSpec as P

MESH = pl.DeviceIdType.MESH

OWN, UP, DOWN = 0, 1, 2


def shifted(x, by):
    width = x.shape[1]
    at = lax.broadcasted_iota(jnp.int32, x.shape, 1)
    edge = 0 if by > 0 else width - 1
    return jnp.where(at == edge, 0.0, pltpu.roll(x, by % width, 1))


def kernel(
    strips, scale, x_ref, g_ref, taps_ref, out_ref, ing_ref, kg_ref,
    x_buf, g_buf, forward, backward, turned, taps_g, whole, pieces, landed, total, send_sem, recv_sem, kg_send, kg_recv, local_sem,
):
    own, height = x_ref.shape[1], x_ref.shape[0]
    channels = x_buf.shape[1]
    width = x_ref.shape[2]
    piece = kg_ref.shape[1]
    row = lax.axis_index("rows")
    chan = lax.axis_index("chan")
    sibling = chan + 1 - 2 * lax.rem(chan, 2)
    across = lax.rem(chan + 2, 4)
    diagonal = lax.rem(sibling + 2, 4)
    of = (chan, sibling, across, diagonal)
    bufs = (x_buf, g_buf)
    last = strips - 1
    span = {OWN: (1, height), UP: (0, 1), DOWN: (height + 1, 1)}

    def region(t, kind, channel):
        start, count = span[kind]
        return bufs[t].at[pl.ds(start, count), pl.ds(pl.multiple_of(channel * own, own), own), :]

    def relay(t, kind, held, to):
        where = region(t, kind, of[held])
        return pltpu.make_async_remote_copy(
            src_ref=where, dst_ref=where,
            send_sem=send_sem.at[t, kind, held ^ to], recv_sem=recv_sem.at[t, kind, held ^ to],
            device_id=(row, of[to]), device_id_type=MESH,
        )

    def edge(t, kind):
        at, to = (height, row + 1) if kind == UP else (1, row - 1)
        return pltpu.make_async_remote_copy(
            src_ref=bufs[t].at[pl.ds(at, 1), pl.ds(pl.multiple_of(chan * own, own), own), :],
            dst_ref=region(t, kind, chan),
            send_sem=send_sem.at[t, kind, 0], recv_sem=recv_sem.at[t, kind, 0],
            device_id=(to, chan), device_id_type=MESH,
        )

    def arrived(t, kind, held):
        where = region(t, kind, of[held])
        pltpu.make_async_remote_copy(
            src_ref=where, dst_ref=where,
            send_sem=send_sem.at[t, kind, held], recv_sem=recv_sem.at[t, kind, held],
            device_id=(row, sibling), device_id_type=MESH,
        ).wait_recv()

    has = {UP: row > 0, DOWN: row < last}
    feeds = {UP: row < last, DOWN: row > 0}

    mine = [
        pltpu.make_async_copy((x_ref, g_ref)[t], region(t, OWN, chan), local_sem.at[t])
        for t in range(2)
    ]
    for copy in mine:
        copy.start()

    barrier = pltpu.get_barrier_semaphore()
    for peer in (sibling, across):
        pl.semaphore_signal(barrier, inc=1, device_id=(row, peer), device_id_type=MESH)

    @pl.loop(1, strips)
    def _(d):
        pl.semaphore_signal(
            barrier, inc=1, device_id=(lax.rem(row + d, strips), chan), device_id_type=MESH
        )

    for kind, at in ((UP, 0), (DOWN, height + 1)):

        @pl.when(jnp.logical_not(has[kind]))
        def _():
            for t in range(2):
                bufs[t][at] = jnp.zeros((channels, width), jnp.bfloat16)

    for copy in mine:
        copy.wait()
    pl.semaphore_wait(barrier, strips + 1)

    def send_edges(t):
        for kind in (UP, DOWN):

            @pl.when(feeds[kind])
            def _():
                edge(t, kind).start()

    def send_own(t):
        relay(t, OWN, 0, 2).start()
        relay(t, OWN, 0, 1).start()

    def relay_edges(t):
        for kind in (UP, DOWN):

            @pl.when(has[kind])
            def _():
                arrived(t, kind, 0)
                relay(t, kind, 0, 2).start()
                relay(t, kind, 0, 1).start()

    def relay_own(t):
        arrived(t, OWN, 2)
        relay(t, OWN, 2, 1).start()

    def pass_on(t):
        for kind in (UP, DOWN):

            @pl.when(has[kind])
            def _():
                arrived(t, kind, 2)
                relay(t, kind, 2, 1).start()

    def complete_own(t):
        arrived(t, OWN, 1)
        arrived(t, OWN, 3)

    def complete_edges(t):
        for kind in (UP, DOWN):

            @pl.when(has[kind])
            def _():
                arrived(t, kind, 1)
                arrived(t, kind, 3)

    def stack(t, h):
        return bufs[t][h : h + 3].reshape(3 * channels, width)

    def convolve(t, w_ref, to_ref):
        for h in range(height):
            terms = jnp.dot(w_ref[...], stack(t, h), preferred_element_type=jnp.float32)
            total = (
                shifted(terms[0:own], 1) + terms[own : 2 * own] + shifted(terms[2 * own : 3 * own], -1)
            )
            to_ref[h] = total.astype(to_ref.dtype)

    send_own(0)
    send_edges(1)
    send_edges(0)
    send_own(1)

    first = pl.multiple_of(chan * own, own)
    pair = pl.multiple_of((chan // 2) * 2 * own, 2 * own)
    for a in range(3):
        for b in range(3):
            at = (3 * a + b) * channels
            forward[b * own : (b + 1) * own, a * channels : (a + 1) * channels] = taps_ref[
                pl.ds(first, own), at : at + channels
            ]
            turned[...] = jnp.transpose(
                taps_ref[:, pl.ds(at + pair, 2 * own)].astype(jnp.float32)
            )
            backward[
                (2 - b) * own : (3 - b) * own, (2 - a) * channels : (3 - a) * channels
            ] = turned[pl.ds(pl.multiple_of(lax.rem(chan, 2) * own, own), own), :].astype(jnp.bfloat16)

    def offset_columns(p, rows):
        wide = rows.astype(jnp.float32)
        taps_g[p, 0:own] = shifted(wide, -1).astype(jnp.bfloat16)
        taps_g[p, own : 2 * own] = rows
        taps_g[p, 2 * own : 3 * own] = shifted(wide, 1).astype(jnp.bfloat16)

    for h in range(height):
        offset_columns(h + 1, g_ref[h])

    relay_own(0)
    relay_edges(1)
    for p in (0, height + 1):
        offset_columns(p, g_buf[p, pl.ds(first, own), :])
    complete_own(0)
    terms = None
    for h in range(height):
        term = lax.dot_general(
            taps_g[h : h + 3].reshape(9 * own, width), x_buf[h + 1],
            (((1,), (1,)), ((), ())), preferred_element_type=jnp.float32,
        )
        terms = term if terms is None else terms + term
    for a in range(3):
        for b in range(3):
            at = (3 * (2 - a) + b) * own
            whole[:, (3 * a + b) * channels : (3 * a + b + 1) * channels] = (
                terms[at : at + own] * scale
            )
    group = pieces.shape[1]
    for s in range(strips):
        for q in range(own // group):
            pieces[s, :, q * piece : (q + 1) * piece] = whole[
                q * group : (q + 1) * group, s * piece : (s + 1) * piece
            ]

    def share(d):
        to = lax.rem(row + d, strips)
        return pltpu.make_async_remote_copy(
            src_ref=pieces.at[to], dst_ref=landed.at[d],
            send_sem=kg_send.at[d], recv_sem=kg_recv.at[d],
            device_id=(to, chan), device_id_type=MESH,
        )

    @pl.loop(1, strips)
    def _(d):
        share(d).start()

    relay_edges(0)
    relay_own(1)
    pass_on(1)
    pass_on(0)
    complete_own(1)
    complete_edges(1)
    convolve(1, backward, ing_ref)
    complete_edges(0)
    convolve(0, forward, out_ref)

    total[...] = pieces[row]

    @pl.loop(1, strips)
    def _(d):
        share(d).wait_recv()
        total[...] += landed[d]

    for q in range(own // group):
        kg_ref[q * group : (q + 1) * group, :] = total[:, q * piece : (q + 1) * piece]

    @pl.loop(1, strips)
    def _(d):
        share(d).wait_send()

    for t in range(2):
        relay(t, OWN, 0, 2).wait_send()
        relay(t, OWN, 0, 1).wait_send()
        relay(t, OWN, 2, 1).wait_send()
        for kind in (UP, DOWN):

            @pl.when(feeds[kind])
            def _():
                edge(t, kind).wait_send()

            @pl.when(has[kind])
            def _():
                relay(t, kind, 0, 2).wait_send()
                relay(t, kind, 0, 1).wait_send()
                relay(t, kind, 2, 1).wait_send()


def body(inputs, kernel_taps, out_grad):
    channels = kernel_taps.shape[0]
    own, height, width = inputs.shape
    strips = lax.axis_size("rows")
    piece = 9 * channels // strips
    splits = [q for q in (1, 2, 4, 8) if own % (8 * q) == 0]
    split = min(splits, key=lambda q: (own // q) * -(-q * piece // 128))
    group, lanes = own // split, split * piece
    scale = 1.0 / math.sqrt(height * strips * width)
    block = jax.ShapeDtypeStruct((height, own, width), jnp.bfloat16)
    vmem = pl.BlockSpec(memory_space=pltpu.VMEM)
    outputs, in_grad, kernel_grad = pl.pallas_call(
        functools.partial(kernel, strips, scale),
        out_shape=(block, block, jax.ShapeDtypeStruct((own, piece), jnp.float32)),
        in_specs=[vmem] * 3,
        out_specs=(vmem,) * 3,
        scratch_shapes=[
            pltpu.VMEM((height + 2, channels, width), jnp.bfloat16),
            pltpu.VMEM((height + 2, channels, width), jnp.bfloat16),
            pltpu.VMEM((3 * own, 3 * channels), jnp.bfloat16),
            pltpu.VMEM((3 * own, 3 * channels), jnp.bfloat16),
            pltpu.VMEM((2 * own, channels), jnp.float32),
            pltpu.VMEM((height + 2, 3 * own, width), jnp.bfloat16),
            pltpu.VMEM((own, 9 * channels), jnp.float32),
            pltpu.VMEM((strips, group, lanes), jnp.float32),
            pltpu.VMEM((strips, group, lanes), jnp.float32),
            pltpu.VMEM((group, lanes), jnp.float32),
            pltpu.SemaphoreType.DMA((2, 3, 4)),
            pltpu.SemaphoreType.DMA((2, 3, 4)),
            pltpu.SemaphoreType.DMA((strips,)),
            pltpu.SemaphoreType.DMA((strips,)),
            pltpu.SemaphoreType.DMA((2,)),
        ],
        compiler_params=pltpu.CompilerParams(
            collective_id=0, has_side_effects=True, vmem_limit_bytes=40 * 1024 * 1024
        ),
    )(jnp.transpose(inputs, (1, 0, 2)), jnp.transpose(out_grad, (1, 0, 2)), kernel_taps)
    return (jnp.transpose(outputs, (1, 0, 2)), jnp.transpose(in_grad, (1, 0, 2)), kernel_grad)


def solution(mesh):
    placed = (P("chan", "rows", None), P(), P("chan", "rows", None))
    return jax.shard_map(
        body,
        mesh=mesh,
        in_specs=placed,
        out_specs=(P("chan", "rows", None), P("chan", "rows", None), P("chan", "rows")),
        check_vma=False,
    )
```

```python
import functools
import math

import jax
import jax.numpy as jnp
from jax import lax
from jax.experimental import pallas as pl
from jax.experimental.pallas import tpu as pltpu
from jax.sharding import PartitionSpec as P

MESH = pl.DeviceIdType.MESH

OWN, UP, DOWN = 0, 1, 2


def shifted(x, by):
    width = x.shape[1]
    at = lax.broadcasted_iota(jnp.int32, x.shape, 1)
    edge = 0 if by > 0 else width - 1
    return jnp.where(at == edge, 0.0, pltpu.roll(x, by % width, 1))


def kernel(
    strips, scale, x_ref, g_ref, taps_hbm, out_ref, ing_ref, kg_ref,
    taps_ref, x_buf, g_buf, forward, backward, turned, taps_g, whole, pieces, landed, total, part, send_sem, recv_sem, kg_send, kg_recv, local_sem, near_sem,
):
    own, height = x_ref.shape[1], x_ref.shape[0]
    channels = x_buf.shape[1]
    width = x_ref.shape[2]
    piece = kg_ref.shape[1]
    row = lax.axis_index("rows")
    chan = lax.axis_index("chan")
    sibling = chan + 1 - 2 * lax.rem(chan, 2)
    across = lax.rem(chan + 2, 4)
    diagonal = lax.rem(sibling + 2, 4)
    of = (chan, sibling, across, diagonal)
    bufs = (x_buf, g_buf)
    last = strips - 1
    span = {OWN: (1, height), UP: (0, 1), DOWN: (height + 1, 1)}

    def region(t, kind, channel):
        start, count = span[kind]
        return bufs[t].at[pl.ds(start, count), pl.ds(pl.multiple_of(channel * own, own), own), :]

    def relay(t, kind, held, to):
        where = region(t, kind, of[held])
        return pltpu.make_async_remote_copy(
            src_ref=where, dst_ref=where,
            send_sem=send_sem.at[t, kind, held ^ to], recv_sem=recv_sem.at[t, kind, held ^ to],
            device_id=(row, of[to]), device_id_type=MESH,
        )

    def edge(t, kind):
        at, to = (height, row + 1) if kind == UP else (1, row - 1)
        return pltpu.make_async_remote_copy(
            src_ref=bufs[t].at[pl.ds(at, 1), pl.ds(pl.multiple_of(chan * own, own), own), :],
            dst_ref=region(t, kind, chan),
            send_sem=send_sem.at[t, kind, 0], recv_sem=recv_sem.at[t, kind, 0],
            device_id=(to, chan), device_id_type=MESH,
        )

    def near_edge(t, kind):
        at, to = (height, row + 1) if kind == UP else (1, row - 1)
        return pltpu.make_async_remote_copy(
            src_ref=bufs[t].at[pl.ds(at, 1), pl.ds(pl.multiple_of(across * own, own), own), :],
            dst_ref=region(t, kind, across),
            send_sem=near_sem.at[t], recv_sem=recv_sem.at[t, kind, 2],
            device_id=(to, chan), device_id_type=MESH,
        )

    def arrived(t, kind, held):
        where = region(t, kind, of[held])
        pltpu.make_async_remote_copy(
            src_ref=where, dst_ref=where,
            send_sem=send_sem.at[t, kind, held], recv_sem=recv_sem.at[t, kind, held],
            device_id=(row, sibling), device_id_type=MESH,
        ).wait_recv()

    has = {UP: row > 0, DOWN: row < last}
    feeds = {UP: row < last, DOWN: row > 0}
    even = lax.rem(row, 2) == 0
    near = {UP: jnp.logical_not(even), DOWN: even}
    nears = {UP: even, DOWN: jnp.logical_not(even)}
    direct = (0,)

    def crosses(t, kind):
        return jnp.logical_and(has[kind], jnp.logical_not(near[kind])) if t in direct else has[kind]

    mine = [
        pltpu.make_async_copy((x_ref, g_ref)[t], region(t, OWN, chan), local_sem.at[t])
        for t in range(2)
    ]
    fetch = pltpu.make_async_copy(taps_hbm, taps_ref, local_sem.at[2])
    for copy in (*mine, fetch):
        copy.start()

    barrier = pltpu.get_barrier_semaphore()
    for peer in (sibling, across):
        pl.semaphore_signal(barrier, inc=1, device_id=(row, peer), device_id_type=MESH)

    @pl.loop(1, strips)
    def _(d):
        pl.semaphore_signal(
            barrier, inc=1, device_id=(lax.rem(row + d, strips), chan), device_id_type=MESH
        )

    for kind, at in ((UP, 0), (DOWN, height + 1)):

        @pl.when(jnp.logical_not(has[kind]))
        def _():
            for t in range(2):
                bufs[t][at] = jnp.zeros((channels, width), jnp.bfloat16)

    for copy in mine:
        copy.wait()
    pl.semaphore_wait(barrier, strips + 1)

    def send_edges(t):
        for kind in (UP, DOWN):

            @pl.when(feeds[kind])
            def _():
                edge(t, kind).start()

    def send_own(t):
        relay(t, OWN, 0, 2).start()
        relay(t, OWN, 0, 1).start()

    def relay_edges(t):
        for kind in (UP, DOWN):

            @pl.when(has[kind])
            def _():
                arrived(t, kind, 0)
                relay(t, kind, 0, 1).start()

            @pl.when(crosses(t, kind))
            def _():
                relay(t, kind, 0, 2).start()

    def relay_own(t):
        arrived(t, OWN, 2)
        relay(t, OWN, 2, 1).start()
        if t in direct:
            for kind in (UP, DOWN):

                @pl.when(nears[kind])
                def _():
                    near_edge(t, kind).start()

    def pass_on(t):
        for kind in (UP, DOWN):

            @pl.when(has[kind])
            def _():
                arrived(t, kind, 2)
                relay(t, kind, 2, 1).start()

    def complete_own(t):
        arrived(t, OWN, 1)
        arrived(t, OWN, 3)

    def complete_edges(t):
        for kind in (UP, DOWN):

            @pl.when(has[kind])
            def _():
                arrived(t, kind, 1)
                arrived(t, kind, 3)

    def from_own(t, w_ref):
        mid = bufs[t][1 : height + 1].reshape(height * channels, width)
        for h in range(height):
            at = (1 - h) * channels
            part[t, h] = jnp.dot(
                w_ref[:, at : at + height * channels], mid, preferred_element_type=jnp.float32
            )

    def from_edges(t, w_ref, to_ref):
        for h in range(height):
            at = 2 * h * channels
            terms = part[t, h] + jnp.dot(
                w_ref[:, at : at + channels], bufs[t][h * (height + 1)],
                preferred_element_type=jnp.float32,
            )
            total = (
                shifted(terms[0:own], 1) + terms[own : 2 * own] + shifted(terms[2 * own : 3 * own], -1)
            )
            to_ref[h] = total.astype(to_ref.dtype)

    send_own(0)
    send_edges(1)
    send_edges(0)
    send_own(1)

    fetch.wait()
    first = pl.multiple_of(chan * own, own)
    pair = pl.multiple_of((chan // 2) * 2 * own, 2 * own)
    for a in range(3):
        for b in range(3):
            at = (3 * a + b) * channels
            forward[b * own : (b + 1) * own, a * channels : (a + 1) * channels] = taps_ref[
                pl.ds(first, own), at : at + channels
            ]
            turned[...] = jnp.transpose(
                taps_ref[:, pl.ds(at + pair, 2 * own)].astype(jnp.float32)
            )
            backward[
                (2 - b) * own : (3 - b) * own, (2 - a) * channels : (3 - a) * channels
            ] = turned[pl.ds(pl.multiple_of(lax.rem(chan, 2) * own, own), own), :].astype(jnp.bfloat16)

    def offset_columns(p, rows):
        wide = rows.astype(jnp.float32)
        taps_g[p, 0:own] = shifted(wide, -1).astype(jnp.bfloat16)
        taps_g[p, own : 2 * own] = rows
        taps_g[p, 2 * own : 3 * own] = shifted(wide, 1).astype(jnp.bfloat16)

    for h in range(height):
        offset_columns(h + 1, g_ref[h])

    relay_own(0)
    relay_edges(1)
    for p in (0, height + 1):
        offset_columns(p, g_buf[p, pl.ds(first, own), :])
    complete_own(0)
    terms = None
    for h in range(height):
        term = lax.dot_general(
            taps_g[h : h + 3].reshape(9 * own, width), x_buf[h + 1],
            (((1,), (1,)), ((), ())), preferred_element_type=jnp.float32,
        )
        terms = term if terms is None else terms + term
    for a in range(3):
        for b in range(3):
            at = (3 * (2 - a) + b) * own
            whole[:, (3 * a + b) * channels : (3 * a + b + 1) * channels] = (
                terms[at : at + own] * scale
            )
    group = pieces.shape[1]
    for s in range(strips):
        for q in range(own // group):
            pieces[s, :, q * piece : (q + 1) * piece] = whole[
                q * group : (q + 1) * group, s * piece : (s + 1) * piece
            ]

    def share(d):
        to = lax.rem(row + d, strips)
        return pltpu.make_async_remote_copy(
            src_ref=pieces.at[to], dst_ref=landed.at[d],
            send_sem=kg_send.at[d], recv_sem=kg_recv.at[d],
            device_id=(to, chan), device_id_type=MESH,
        )

    @pl.loop(1, strips)
    def _(d):
        share(d).start()

    relay_edges(0)
    relay_own(1)
    from_own(0, forward)
    pass_on(1)
    complete_own(1)
    pass_on(0)
    from_own(1, backward)
    complete_edges(1)
    from_edges(1, backward, ing_ref)

    complete_edges(0)
    from_edges(0, forward, out_ref)

    total[...] = pieces[row]

    @pl.loop(1, strips)
    def _(d):
        share(d).wait_recv()
        total[...] += landed[d]

    for q in range(own // group):
        kg_ref[q * group : (q + 1) * group, :] = total[:, q * piece : (q + 1) * piece]

    @pl.loop(1, strips)
    def _(d):
        share(d).wait_send()

    for t in range(2):
        relay(t, OWN, 0, 2).wait_send()
        relay(t, OWN, 0, 1).wait_send()
        relay(t, OWN, 2, 1).wait_send()
        for kind in (UP, DOWN):

            @pl.when(feeds[kind])
            def _():
                edge(t, kind).wait_send()

            @pl.when(crosses(t, kind))
            def _():
                relay(t, kind, 0, 2).wait_send()

            if t in direct:

                @pl.when(nears[kind])
                def _():
                    near_edge(t, kind).wait_send()

            @pl.when(has[kind])
            def _():
                relay(t, kind, 0, 1).wait_send()
                relay(t, kind, 2, 1).wait_send()


def body(inputs, kernel_taps, out_grad):
    channels = kernel_taps.shape[0]
    own, height, width = inputs.shape
    strips = lax.axis_size("rows")
    piece = 9 * channels // strips
    splits = [q for q in (1, 2, 4, 8) if own % (8 * q) == 0]
    split = min(splits, key=lambda q: (own // q) * -(-q * piece // 128))
    group, lanes = own // split, split * piece
    scale = 1.0 / math.sqrt(height * strips * width)
    block = jax.ShapeDtypeStruct((height, own, width), jnp.bfloat16)
    vmem = pl.BlockSpec(memory_space=pltpu.VMEM)
    outputs, in_grad, kernel_grad = pl.pallas_call(
        functools.partial(kernel, strips, scale),
        out_shape=(block, block, jax.ShapeDtypeStruct((own, piece), jnp.float32)),
        in_specs=[vmem, vmem, pl.BlockSpec(memory_space=pltpu.HBM)],
        out_specs=(vmem,) * 3,
        scratch_shapes=[
            pltpu.VMEM(kernel_taps.shape, jnp.bfloat16),
            pltpu.VMEM((height + 2, channels, width), jnp.bfloat16),
            pltpu.VMEM((height + 2, channels, width), jnp.bfloat16),
            pltpu.VMEM((3 * own, 3 * channels), jnp.bfloat16),
            pltpu.VMEM((3 * own, 3 * channels), jnp.bfloat16),
            pltpu.VMEM((2 * own, channels), jnp.float32),
            pltpu.VMEM((height + 2, 3 * own, width), jnp.bfloat16),
            pltpu.VMEM((own, 9 * channels), jnp.float32),
            pltpu.VMEM((strips, group, lanes), jnp.float32),
            pltpu.VMEM((strips, group, lanes), jnp.float32),
            pltpu.VMEM((group, lanes), jnp.float32),
            pltpu.VMEM((2, height, 3 * own, width), jnp.float32),
            pltpu.SemaphoreType.DMA((2, 3, 4)),
            pltpu.SemaphoreType.DMA((2, 3, 4)),
            pltpu.SemaphoreType.DMA((strips,)),
            pltpu.SemaphoreType.DMA((strips,)),
            pltpu.SemaphoreType.DMA((3,)),
            pltpu.SemaphoreType.DMA((2,)),
        ],
        compiler_params=pltpu.CompilerParams(
            collective_id=0, has_side_effects=True, vmem_limit_bytes=40 * 1024 * 1024
        ),
    )(jnp.transpose(inputs, (1, 0, 2)), jnp.transpose(out_grad, (1, 0, 2)), kernel_taps)
    return (jnp.transpose(outputs, (1, 0, 2)), jnp.transpose(in_grad, (1, 0, 2)), kernel_grad)


def solution(mesh):
    placed = (P("chan", "rows", None), P(), P("chan", "rows", None))
    return jax.shard_map(
        body,
        mesh=mesh,
        in_specs=placed,
        out_specs=(P("chan", "rows", None), P("chan", "rows", None), P("chan", "rows")),
        check_vma=False,
    )
```

```python
import functools
import math

import jax
import jax.numpy as jnp
from jax import lax
from jax.experimental import pallas as pl
from jax.experimental.pallas import tpu as pltpu
from jax.sharding import PartitionSpec as P

MESH = pl.DeviceIdType.MESH

OWN, UP, DOWN = 0, 1, 2


def shifted(x, by):
    width = x.shape[1]
    at = lax.broadcasted_iota(jnp.int32, x.shape, 1)
    edge = 0 if by > 0 else width - 1
    return jnp.where(at == edge, 0.0, pltpu.roll(x, by % width, 1))


def kernel(
    strips, scale, x_ref, g_ref, taps_hbm, out_ref, ing_ref, kg_ref,
    taps_ref, x_buf, g_buf, forward, backward, turned, taps_g, whole, pieces, landed, total, part, send_sem, recv_sem, kg_send, kg_recv, local_sem, near_sem,
):
    own, height = x_ref.shape[1], x_ref.shape[0]
    channels = x_buf.shape[1]
    width = x_ref.shape[2]
    piece = kg_ref.shape[1]
    row = lax.axis_index("rows")
    chan = lax.axis_index("chan")
    sibling = chan + 1 - 2 * lax.rem(chan, 2)
    across = lax.rem(chan + 2, 4)
    diagonal = lax.rem(sibling + 2, 4)
    of = (chan, sibling, across, diagonal)
    bufs = (x_buf, g_buf)
    last = strips - 1
    span = {OWN: (1, height), UP: (0, 1), DOWN: (height + 1, 1)}

    def region(t, kind, channel):
        start, count = span[kind]
        return bufs[t].at[pl.ds(start, count), pl.ds(pl.multiple_of(channel * own, own), own), :]

    def relay(t, kind, held, to):
        where = region(t, kind, of[held])
        return pltpu.make_async_remote_copy(
            src_ref=where, dst_ref=where,
            send_sem=send_sem.at[t, kind, held ^ to], recv_sem=recv_sem.at[t, kind, held ^ to],
            device_id=(row, of[to]), device_id_type=MESH,
        )

    def edge(t, kind):
        at, to = (height, row + 1) if kind == UP else (1, row - 1)
        return pltpu.make_async_remote_copy(
            src_ref=bufs[t].at[pl.ds(at, 1), pl.ds(pl.multiple_of(chan * own, own), own), :],
            dst_ref=region(t, kind, chan),
            send_sem=send_sem.at[t, kind, 0], recv_sem=recv_sem.at[t, kind, 0],
            device_id=(to, chan), device_id_type=MESH,
        )

    def near_edge(t, kind):
        at, to = (height, row + 1) if kind == UP else (1, row - 1)
        return pltpu.make_async_remote_copy(
            src_ref=bufs[t].at[pl.ds(at, 1), pl.ds(pl.multiple_of(across * own, own), own), :],
            dst_ref=region(t, kind, across),
            send_sem=near_sem.at[t], recv_sem=recv_sem.at[t, kind, 2],
            device_id=(to, chan), device_id_type=MESH,
        )

    def arrived(t, kind, held):
        where = region(t, kind, of[held])
        pltpu.make_async_remote_copy(
            src_ref=where, dst_ref=where,
            send_sem=send_sem.at[t, kind, held], recv_sem=recv_sem.at[t, kind, held],
            device_id=(row, sibling), device_id_type=MESH,
        ).wait_recv()

    has = {UP: row > 0, DOWN: row < last}
    feeds = {UP: row < last, DOWN: row > 0}
    even = lax.rem(row, 2) == 0
    near = {UP: jnp.logical_not(even), DOWN: even}
    nears = {UP: even, DOWN: jnp.logical_not(even)}
    direct = (0,)

    def crosses(t, kind):
        return jnp.logical_and(has[kind], jnp.logical_not(near[kind])) if t in direct else has[kind]

    mine = [
        pltpu.make_async_copy((x_ref, g_ref)[t], region(t, OWN, chan), local_sem.at[t])
        for t in range(2)
    ]
    fetch = pltpu.make_async_copy(taps_hbm, taps_ref, local_sem.at[2])
    for copy in (*mine, fetch):
        copy.start()

    barrier = pltpu.get_barrier_semaphore()
    for peer in (sibling, across):
        pl.semaphore_signal(barrier, inc=1, device_id=(row, peer), device_id_type=MESH)

    @pl.loop(1, strips)
    def _(d):
        pl.semaphore_signal(
            barrier, inc=1, device_id=(lax.rem(row + d, strips), chan), device_id_type=MESH
        )

    for kind, at in ((UP, 0), (DOWN, height + 1)):

        @pl.when(jnp.logical_not(has[kind]))
        def _():
            for t in range(2):
                bufs[t][at] = jnp.zeros((channels, width), jnp.bfloat16)

    for copy in mine:
        copy.wait()
    pl.semaphore_wait(barrier, strips + 1)

    def send_edges(t):
        for kind in (UP, DOWN):

            @pl.when(feeds[kind])
            def _():
                edge(t, kind).start()

    def send_own(t):
        relay(t, OWN, 0, 2).start()
        relay(t, OWN, 0, 1).start()

    def relay_edges(t):
        for kind in (UP, DOWN):

            @pl.when(has[kind])
            def _():
                arrived(t, kind, 0)
                relay(t, kind, 0, 1).start()

            @pl.when(crosses(t, kind))
            def _():
                relay(t, kind, 0, 2).start()

    def relay_own(t):
        arrived(t, OWN, 2)
        relay(t, OWN, 2, 1).start()
        if t in direct:
            for kind in (UP, DOWN):

                @pl.when(nears[kind])
                def _():
                    near_edge(t, kind).start()

    def pass_on(t):
        for kind in (UP, DOWN):

            @pl.when(has[kind])
            def _():
                arrived(t, kind, 2)
                relay(t, kind, 2, 1).start()

    def complete_own(t):
        arrived(t, OWN, 1)
        arrived(t, OWN, 3)

    def complete_edges(t):
        for kind in (UP, DOWN):

            @pl.when(has[kind])
            def _():
                arrived(t, kind, 1)
                arrived(t, kind, 3)

    def from_own(t, w_ref):
        mid = bufs[t][1 : height + 1].reshape(height * channels, width)
        for h in range(height):
            at = (1 - h) * channels
            part[t, h] = jnp.dot(
                w_ref[:, at : at + height * channels], mid, preferred_element_type=jnp.float32
            )

    def from_edges(t, w_ref, to_ref):
        for h in range(height):
            at = 2 * h * channels
            terms = part[t, h] + jnp.dot(
                w_ref[:, at : at + channels], bufs[t][h * (height + 1)],
                preferred_element_type=jnp.float32,
            )
            total = (
                shifted(terms[0:own], 1) + terms[own : 2 * own] + shifted(terms[2 * own : 3 * own], -1)
            )
            to_ref[h] = total.astype(to_ref.dtype)

    send_edges(1)
    send_own(0)
    send_edges(0)
    send_own(1)

    fetch.wait()
    first = pl.multiple_of(chan * own, own)
    pair = pl.multiple_of((chan // 2) * 2 * own, 2 * own)
    for a in range(3):
        for b in range(3):
            at = (3 * a + b) * channels
            forward[b * own : (b + 1) * own, a * channels : (a + 1) * channels] = taps_ref[
                pl.ds(first, own), at : at + channels
            ]
            turned[...] = jnp.transpose(
                taps_ref[:, pl.ds(at + pair, 2 * own)].astype(jnp.float32)
            )
            backward[
                (2 - b) * own : (3 - b) * own, (2 - a) * channels : (3 - a) * channels
            ] = turned[pl.ds(pl.multiple_of(lax.rem(chan, 2) * own, own), own), :].astype(jnp.bfloat16)

    def offset_columns(p, rows):
        wide = rows.astype(jnp.float32)
        taps_g[p, 0:own] = shifted(wide, -1).astype(jnp.bfloat16)
        taps_g[p, own : 2 * own] = rows
        taps_g[p, 2 * own : 3 * own] = shifted(wide, 1).astype(jnp.bfloat16)

    for h in range(height):
        offset_columns(h + 1, g_ref[h])

    relay_own(0)
    relay_edges(1)
    for p in (0, height + 1):
        offset_columns(p, g_buf[p, pl.ds(first, own), :])
    complete_own(0)
    terms = None
    for h in range(height):
        term = lax.dot_general(
            taps_g[h : h + 3].reshape(9 * own, width), x_buf[h + 1],
            (((1,), (1,)), ((), ())), preferred_element_type=jnp.float32,
        )
        terms = term if terms is None else terms + term
    for a in range(3):
        for b in range(3):
            at = (3 * (2 - a) + b) * own
            whole[:, (3 * a + b) * channels : (3 * a + b + 1) * channels] = (
                terms[at : at + own] * scale
            )
    group = pieces.shape[1]
    for s in range(strips):
        for q in range(own // group):
            pieces[s, :, q * piece : (q + 1) * piece] = whole[
                q * group : (q + 1) * group, s * piece : (s + 1) * piece
            ]

    def share(d):
        to = lax.rem(row + d, strips)
        return pltpu.make_async_remote_copy(
            src_ref=pieces.at[to], dst_ref=landed.at[d],
            send_sem=kg_send.at[d], recv_sem=kg_recv.at[d],
            device_id=(to, chan), device_id_type=MESH,
        )

    @pl.loop(1, strips)
    def _(d):
        share(d).start()

    relay_edges(0)
    relay_own(1)
    pass_on(1)
    from_own(0, forward)
    complete_own(1)
    from_own(1, backward)
    pass_on(0)
    complete_edges(1)
    from_edges(1, backward, ing_ref)

    complete_edges(0)
    from_edges(0, forward, out_ref)

    total[...] = pieces[row]

    @pl.loop(1, strips)
    def _(d):
        share(d).wait_recv()
        total[...] += landed[d]

    for q in range(own // group):
        kg_ref[q * group : (q + 1) * group, :] = total[:, q * piece : (q + 1) * piece]

    @pl.loop(1, strips)
    def _(d):
        share(d).wait_send()

    for t in range(2):
        relay(t, OWN, 0, 2).wait_send()
        relay(t, OWN, 0, 1).wait_send()
        relay(t, OWN, 2, 1).wait_send()
        for kind in (UP, DOWN):

            @pl.when(feeds[kind])
            def _():
                edge(t, kind).wait_send()

            @pl.when(crosses(t, kind))
            def _():
                relay(t, kind, 0, 2).wait_send()

            if t in direct:

                @pl.when(nears[kind])
                def _():
                    near_edge(t, kind).wait_send()

            @pl.when(has[kind])
            def _():
                relay(t, kind, 0, 1).wait_send()
                relay(t, kind, 2, 1).wait_send()


def body(inputs, kernel_taps, out_grad):
    channels = kernel_taps.shape[0]
    own, height, width = inputs.shape
    strips = lax.axis_size("rows")
    piece = 9 * channels // strips
    splits = [q for q in (1, 2, 4, 8) if own % (8 * q) == 0]
    split = min(splits, key=lambda q: (own // q) * -(-q * piece // 128))
    group, lanes = own // split, split * piece
    scale = 1.0 / math.sqrt(height * strips * width)
    block = jax.ShapeDtypeStruct((height, own, width), jnp.bfloat16)
    vmem = pl.BlockSpec(memory_space=pltpu.VMEM)
    outputs, in_grad, kernel_grad = pl.pallas_call(
        functools.partial(kernel, strips, scale),
        out_shape=(block, block, jax.ShapeDtypeStruct((own, piece), jnp.float32)),
        in_specs=[vmem, vmem, pl.BlockSpec(memory_space=pltpu.HBM)],
        out_specs=(vmem,) * 3,
        scratch_shapes=[
            pltpu.VMEM(kernel_taps.shape, jnp.bfloat16),
            pltpu.VMEM((height + 2, channels, width), jnp.bfloat16),
            pltpu.VMEM((height + 2, channels, width), jnp.bfloat16),
            pltpu.VMEM((3 * own, 3 * channels), jnp.bfloat16),
            pltpu.VMEM((3 * own, 3 * channels), jnp.bfloat16),
            pltpu.VMEM((2 * own, channels), jnp.float32),
            pltpu.VMEM((height + 2, 3 * own, width), jnp.bfloat16),
            pltpu.VMEM((own, 9 * channels), jnp.float32),
            pltpu.VMEM((strips, group, lanes), jnp.float32),
            pltpu.VMEM((strips, group, lanes), jnp.float32),
            pltpu.VMEM((group, lanes), jnp.float32),
            pltpu.VMEM((2, height, 3 * own, width), jnp.float32),
            pltpu.SemaphoreType.DMA((2, 3, 4)),
            pltpu.SemaphoreType.DMA((2, 3, 4)),
            pltpu.SemaphoreType.DMA((strips,)),
            pltpu.SemaphoreType.DMA((strips,)),
            pltpu.SemaphoreType.DMA((3,)),
            pltpu.SemaphoreType.DMA((2,)),
        ],
        compiler_params=pltpu.CompilerParams(
            collective_id=0, has_side_effects=True, vmem_limit_bytes=40 * 1024 * 1024
        ),
    )(jnp.transpose(inputs, (1, 0, 2)), jnp.transpose(out_grad, (1, 0, 2)), kernel_taps)
    return (jnp.transpose(outputs, (1, 0, 2)), jnp.transpose(in_grad, (1, 0, 2)), kernel_grad)


def solution(mesh):
    placed = (P("chan", "rows", None), P(), P("chan", "rows", None))
    return jax.shard_map(
        body,
        mesh=mesh,
        in_specs=placed,
        out_specs=(P("chan", "rows", None), P("chan", "rows", None), P("chan", "rows")),
        check_vma=False,
    )
```
